32 devices in a mesh: groups: 2 (over y), row: 8 (over z, x), col: 2 (over core).
Axes of the slice: x: 2, y: 2, z: 4, core: 2. Of those that a mesh axis runs over, the one named last changes fastest.
Arguments:
- src_emb: bfloat16 [8192, 128], P(('groups', 'row', 'col')), parts along dimension 0, may hold values from -6 to 6
- tgt_emb: bfloat16 [65536, 128], P(('groups', 'col', 'row')), parts along dimension 0, may hold values from -6 to 6
- src_scale: float32 [8192], P(('groups', 'row', 'col')), parts along dimension 0, may hold values from 0.5 to 1.5
- tgt_scale: float32 [65536], P(('groups', 'col', 'row')), parts along dimension 0, may hold values from 0.5 to 1.5
- src_mass: float32 [8192], P(('groups', 'row')), parts along dimension 0, may hold values from 0.05 to 20
- tgt_mass: float32 [65536], P(('groups', 'col')), parts along dimension 0, may hold values from 0.05 to 20
Outputs:
- src_potential: float32 [8192], P(('groups', 'row')), parts along dimension 0
- tgt_potential: float32 [65536], P(('groups', 'col')), parts along dimension 0
The draws below stay inside these ranges and needn't reach their ends.
There are 2 independent parts, one for each index of `groups`. The reference program is written for one: setup_inputs(seed, part) draws one part's arguments, and reference() takes and returns one part's arrays. A program takes and returns all parts, laid end to end along the dimension named above; each array names one. Nothing has to cross between parts.
All inputs are finite; a program needn't handle non-finite values.
Results may differ from the reference program's by a relative error of at most 0.00056.
Values may be sent and summed in bfloat16 or wider, within the bound.
A program may use at most 64 MiB of HBM per device.

```python
import math
import jax
import jax.numpy as jnp
from jax import lax

FEAT = 128
SRC_DEV = 512
ITERS = 3
NS = 4096
NT = 32768
N_ROW = 8


def shard_levels(rng, extent, split, smallest, high):
    factor_of = 1.0
    for position, shards_of in split:
        heights = jax.random.uniform(jax.random.fold_in(jax.random.fold_in(rng, 6), position), (shards_of,), jnp.float32, smallest / len(split), high / len(split))
        factor_of = factor_of * jnp.repeat(jnp.exp(heights), extent[position] // shards_of).reshape((-1,) + (1,) * (len(extent) - 1 - position))
    return factor_of


def normal_values(own_key, extent, deviation, limit, cuts=(), kind=jnp.bfloat16):
    factor_of = shard_levels(own_key, extent, cuts, -0.22, 0.18) if cuts else 1.0
    array = jax.random.normal(own_key, extent, jnp.float32) * deviation * factor_of
    return jnp.minimum(jnp.maximum(array, -limit), limit).astype(kind)


def setup_inputs(seed: int = 0, part: int = 0) -> dict:
    key_of = jax.random.split(jax.random.key(seed), 7)
    own_keys = jax.random.split(jax.random.fold_in(key_of[6], part), 7)
    return {
        "src_emb": normal_values(own_keys[0], (NS, FEAT), 1.0, 6.0, ((0, 16),)),
        "tgt_emb": normal_values(own_keys[1], (NT, FEAT), 1.0, 6.0, ((0, 16),)),
        "src_scale": jnp.clip(jnp.exp(math.log(1.5) - 1.0986123 * jax.random.uniform(own_keys[2], (NS,), jnp.float32) ** shard_levels(own_keys[2], (NS,), ((0, 16),), -0.2, 0.2)), 0.5, 1.5),
        "tgt_scale": jnp.clip(jnp.exp(math.log(1.5) - 1.0986123 * jax.random.uniform(own_keys[3], (NT,), jnp.float32) ** shard_levels(own_keys[3], (NT,), ((0, 16),), -0.2, 0.2)), 0.5, 1.5),
        "src_mass": jnp.clip(jnp.exp(math.log(20.0) - 5.9914645 * jax.random.uniform(own_keys[4], (NS,), jnp.float32) ** shard_levels(own_keys[4], (NS,), ((0, 8),), -0.2, 0.2)), 0.05, 20.0),
        "tgt_mass": jnp.clip(jnp.exp(math.log(20.0) - 5.9914645 * jax.random.uniform(own_keys[5], (NT,), jnp.float32) ** shard_levels(own_keys[5], (NT,), ((0, 2),), -0.2, 0.2)), 0.05, 20.0),
    }


EPSILON = 0.05

def unit_rows(emb, scale):
    values = emb.astype(jnp.float32)
    length = jnp.sqrt(lax.optimization_barrier(jnp.sum(values * values, axis=1)) + 1e-06)
    return (values * (scale / length)[:, None]).astype(jnp.bfloat16)

def reference(src_emb, tgt_emb, src_scale, tgt_scale, src_mass, tgt_mass):
    src_unit = unit_rows(src_emb, src_scale)
    tgt_unit = unit_rows(tgt_emb, tgt_scale)
    src_blocks = src_unit.reshape(N_ROW, SRC_DEV, FEAT)

    def tile(block):
        return jnp.exp(jnp.dot(block, tgt_unit.T, preferred_element_type=jnp.float32) / EPSILON).astype(jnp.bfloat16)
    right_scaling = jnp.ones((NT,), jnp.float32)
    left_scaling = jnp.ones((NS,), jnp.float32)
    for step in range(ITERS):
        right_low = right_scaling.astype(jnp.bfloat16)
        totals = lax.map(lambda block: jnp.dot(tile(block), right_low, preferred_element_type=jnp.float32), src_blocks)
        left_scaling = src_mass / totals.reshape(NS)
        left_low = left_scaling.astype(jnp.bfloat16).reshape(N_ROW, SRC_DEV)

        def add_block(total, pair):
            block, weights = pair
            return (total + jnp.dot(weights, tile(block), preferred_element_type=jnp.float32), None)
        col_totals, unused = lax.scan(add_block, jnp.zeros((NT,), jnp.float32), (src_blocks, left_low))
        right_scaling = tgt_mass / col_totals
    return (EPSILON * jnp.log(left_scaling), EPSILON * jnp.log(right_scaling))
```

```python
import jax
import jax.numpy as jnp
from jax import lax
from jax.sharding import PartitionSpec as P

ITERS = 3


EPSILON = 0.05


def unit_rows(emb, scale):
    values = emb.astype(jnp.float32)
    length = jnp.sqrt(jnp.sum(values * values, axis=1) + 1e-06)
    return (values * (scale / length)[:, None]).astype(jnp.bfloat16)


def body(src_emb, tgt_emb, src_scale, tgt_scale, src_mass, tgt_mass):
    both = ("row", "col")
    src_all = lax.all_gather(unit_rows(src_emb, src_scale), both, axis=0, tiled=True)
    mass_all = lax.all_gather(src_mass, "row", axis=0, tiled=True)
    tgt_unit = unit_rows(tgt_emb, tgt_scale)
    own = tgt_unit.shape[0]
    row = lax.axis_index("row")
    mass_own = lax.dynamic_slice(tgt_mass, (row * own,), (own,))
    scores = lax.dot_general(
        src_all, tgt_unit, (((1,), (1,)), ((), ())), preferred_element_type=jnp.float32
    )
    kernel = jnp.exp(scores / EPSILON).astype(jnp.bfloat16)
    right_scaling = jnp.ones((own,), jnp.float32)
    for step in range(ITERS):
        partial_rows = jnp.dot(
            kernel, right_scaling.astype(jnp.bfloat16), preferred_element_type=jnp.float32
        )
        left_scaling = mass_all / lax.psum(partial_rows, both)
        cols = jnp.dot(
            left_scaling.astype(jnp.bfloat16), kernel, preferred_element_type=jnp.float32
        )
        right_scaling = mass_own / cols
    rows_own = src_mass.shape[0]
    left_own = lax.dynamic_slice(left_scaling, (row * rows_own,), (rows_own,))
    right_all = lax.all_gather(EPSILON * jnp.log(right_scaling), "row", axis=0, tiled=True)
    return (EPSILON * jnp.log(left_own), right_all)


def solution(mesh):
    in_specs = (
        P(("groups", "row", "col"), None),
        P(("groups", "col", "row"), None),
        P(("groups", "row", "col")),
        P(("groups", "col", "row")),
        P(("groups", "row")),
        P(("groups", "col")),
    )
    out_specs = (P(("groups", "row")), P(("groups", "col")))
    return jax.shard_map(body, mesh=mesh, in_specs=in_specs, out_specs=out_specs, check_vma=False)
```

```python
import functools
import jax
import jax.numpy as jnp
from jax import lax
from jax.experimental import pallas as pl
from jax.experimental.pallas import tpu as pltpu
from jax.sharding import PartitionSpec as P

ITERS = 3


EPSILON = 0.05
LOG2_E = 1.4426950408889634
MESH = pl.DeviceIdType.MESH
F32 = jnp.float32
BF16 = jnp.bfloat16


def unit_rows(emb, scale):
    values = emb.astype(F32)
    length = jnp.sqrt(jnp.sum(values * values, axis=1) + 1e-06)
    return (values * (scale / length)[:, None]).astype(BF16)


def lanes_to_row(acc):
    high = acc.astype(BF16)
    low = (acc - high.astype(F32)).astype(BF16)
    both = jnp.concatenate([high, low], axis=1)
    ones = jnp.ones((8, both.shape[1]), BF16)
    return lax.dot_general(
        ones, both, (((1,), (1,)), ((), ())), preferred_element_type=F32
    )


def sinkhorn(
    n_row, n_col,
    src_ref, tgt_ref, src_mass_ref, tgt_mass_ref,
    src_out, tgt_out,
    src_all, kernel, part, inbox, left, right,
    gather_send, gather_recv, sum_send, sum_recv, left_send, left_recv, out_send, out_recv,
):
    n_dev = n_row * n_col
    row, col = lax.axis_index("row"), lax.axis_index("col")
    me = row * n_col + col
    size = src_ref.shape[0]
    own = tgt_ref.shape[0]

    def rows_of(q):
        return pl.ds(pl.multiple_of(q * size, size), size)

    def after(k):
        return lax.rem(me + k, n_dev)

    def before(k):
        return lax.rem(me - k + n_dev, n_dev)

    def peer(q):
        return {"row": q // n_col, "col": lax.rem(q, n_col)}

    def copy(src, dst, send, recv, device):
        return pltpu.make_async_remote_copy(
            src_ref=src, dst_ref=dst, send_sem=send, recv_sem=recv,
            device_id=device, device_id_type=MESH,
        )

    def gather_copy(q, origin):
        return copy(src_ref, src_all.at[rows_of(origin), :],
                    gather_send.at[q], gather_recv.at[origin], peer(q))

    def sum_copy(q, origin):
        return copy(part.at[:, rows_of(q)], inbox.at[origin],
                    sum_send.at[q], sum_recv.at[origin], peer(q))

    def left_copy(q, origin):
        return copy(left.at[:, rows_of(origin)], left.at[:, rows_of(origin)],
                    left_send.at[q], left_recv.at[origin], peer(q))

    barrier = pltpu.get_barrier_semaphore()

    @pl.loop(1, n_dev)
    def _(k):
        pl.semaphore_signal(barrier, inc=1, device_id=peer(after(k)), device_id_type=MESH)

    pl.semaphore_wait(barrier, n_dev - 1)

    @pl.loop(1, n_dev)
    def _(k):
        q = after(k)
        gather_copy(q, me).start()

    def lane_sums(tile_of):
        acc = tile_of(0)
        for j in range(1, own // 128):
            acc = acc + tile_of(j)
        return acc

    def make_tile(block, q):
        scores = lax.dot_general(
            block, tgt_ref[...], (((1,), (1,)), ((), ())), preferred_element_type=F32
        )
        tile = jnp.exp2(scores * (LOG2_E / EPSILON)).astype(BF16)
        kernel[rows_of(q), :] = tile
        tile = tile.astype(F32)
        acc = lane_sums(lambda j: tile[:, j * 128:(j + 1) * 128])
        return lanes_to_row(acc)[0:1, :]

    def weigh_tile(q):
        acc = lane_sums(
            lambda j: kernel[rows_of(q), j * 128:(j + 1) * 128].astype(F32)
            * right[:, j * 128:(j + 1) * 128]
        )
        return lanes_to_row(acc)[0:1, :]

    def finish_left():
        @pl.loop(1, n_dev)
        def _(k):
            q = before(k)
            sum_copy(q, q).wait_recv()

        total = jnp.sum(inbox[...], axis=0)
        mass = src_mass_ref[:, pl.ds(pl.multiple_of(col * size, size), size)]
        left[:, rows_of(me)] = mass / total

        @pl.loop(1, n_dev)
        def _(k):
            left_copy(after(k), me).start()

        @pl.loop(1, n_dev)
        def _(k):
            q = before(k)
            left_copy(q, q).wait_recv()

        @pl.loop(1, n_dev)
        def _(k):
            q = after(k)
            sum_copy(q, me).wait_send()
            left_copy(q, me).wait_send()

    def right_scaling():
        weights = jnp.broadcast_to(left[...].astype(BF16), (8, left.shape[1]))
        cols = jnp.dot(weights, kernel[...], preferred_element_type=F32)
        mass = tgt_mass_ref[:, pl.ds(pl.multiple_of(row * own, own), own)]
        return mass / cols[0:1, :]

    inbox[me] = make_tile(src_ref[...], me)

    @pl.loop(1, n_dev)
    def _(k):
        q = before(k)
        gather_copy(q, q).wait_recv()
        part[:, rows_of(q)] = make_tile(src_all[rows_of(q), :], q)
        sum_copy(q, me).start()

    @pl.loop(1, n_dev)
    def _(k):
        gather_copy(after(k), me).wait_send()

    finish_left()

    @pl.loop(1, ITERS)
    def _(step):
        right[...] = right_scaling().astype(BF16).astype(F32)

        @pl.loop(1, n_dev)
        def _(k):
            q = before(k)
            part[:, rows_of(q)] = weigh_tile(q)
            sum_copy(q, me).start()

        inbox[me] = weigh_tile(me)
        finish_left()

    def out_block(r):
        return tgt_out.at[:, pl.ds(pl.multiple_of(r * own, own), own)]

    def out_copy(r, origin):
        return copy(out_block(origin), out_block(origin),
                    out_send.at[r], out_recv.at[origin], {"row": r, "col": col})

    tgt_out[:, pl.ds(pl.multiple_of(row * own, own), own)] = EPSILON * jnp.log(right_scaling())

    @pl.loop(1, n_row)
    def _(k):
        out_copy(lax.rem(row + k, n_row), row).start()

    span = n_col * size
    src_out[...] = EPSILON * jnp.log(left[:, pl.ds(pl.multiple_of(row * span, span), span)])

    @pl.loop(1, n_row)
    def _(k):
        r = lax.rem(row - k + n_row, n_row)
        out_copy(r, r).wait_recv()
        out_copy(lax.rem(row + k, n_row), row).wait_send()


def body(n_row, n_col, src_emb, tgt_emb, src_scale, tgt_scale, src_mass, tgt_mass):
    src_unit = unit_rows(src_emb, src_scale)
    tgt_unit = unit_rows(tgt_emb, tgt_scale)
    n_dev = n_row * n_col
    size, feat = src_emb.shape
    own = tgt_emb.shape[0]
    total = n_dev * size
    vmem = pl.BlockSpec(memory_space=pltpu.VMEM)
    dma = pltpu.SemaphoreType.DMA
    src_potential, tgt_potential = pl.pallas_call(
        functools.partial(sinkhorn, n_row, n_col),
        out_shape=(
            jax.ShapeDtypeStruct((1, n_col * size), F32),
            jax.ShapeDtypeStruct((1, n_row * own), F32),
        ),
        in_specs=[vmem] * 4,
        out_specs=(vmem, vmem),
        scratch_shapes=[
            pltpu.VMEM((total, feat), BF16),
            pltpu.VMEM((total, own), BF16),
            pltpu.VMEM((1, total), F32),
            pltpu.VMEM((n_dev, 1, size), F32),
            pltpu.VMEM((1, total), F32),
            pltpu.VMEM((1, own), F32),
            dma((n_dev,)), dma((n_dev,)), dma((n_dev,)), dma((n_dev,)),
            dma((n_dev,)), dma((n_dev,)), dma((n_row,)), dma((n_row,)),
        ],
        compiler_params=pltpu.CompilerParams(
            collective_id=0, has_side_effects=True, vmem_limit_bytes=56 * 2**20
        ),
        name="sinkhorn",
    )(src_unit, tgt_unit, src_mass[None, :], tgt_mass[None, :])
    return src_potential[0], tgt_potential[0]


def solution(mesh):
    in_specs = (
        P(("groups", "row", "col"), None),
        P(("groups", "col", "row"), None),
        P(("groups", "row", "col")),
        P(("groups", "col", "row")),
        P(("groups", "row")),
        P(("groups", "col")),
    )
    out_specs = (P(("groups", "row")), P(("groups", "col")))
    step = functools.partial(body, mesh.shape["row"], mesh.shape["col"])
    return jax.shard_map(step, mesh=mesh, in_specs=in_specs, out_specs=out_specs, check_vma=False)
```

```python
import functools
import jax
import jax.numpy as jnp
from jax import lax
from jax.experimental import pallas as pl
from jax.experimental.pallas import tpu as pltpu
from jax.sharding import PartitionSpec as P

ITERS = 3


EPSILON = 0.05
LOG2_E = 1.4426950408889634
MESH = pl.DeviceIdType.MESH
F32 = jnp.float32
BF16 = jnp.bfloat16


def lanes_to_row(acc):
    high = acc.astype(BF16)
    low = (acc - high.astype(F32)).astype(BF16)
    both = jnp.concatenate([high, low], axis=1)
    ones = jnp.ones((8, both.shape[1]), BF16)
    return lax.dot_general(
        ones, both, (((1,), (1,)), ((), ())), preferred_element_type=F32
    )


def sinkhorn(
    n_row, n_col,
    src_ref, tgt_ref, src_scale_ref, tgt_scale_ref, src_mass_ref, tgt_mass_ref,
    src_out, tgt_out,
    src_all, tgt_all, kernel, part, inbox, left, right,
    far_send, low_send, col_send, gather_recv, sum_send, sum_recv, left_send, left_recv, out_send, out_recv,
):
    n_dev = n_row * n_col
    row, col = lax.axis_index("row"), lax.axis_index("col")
    n_low = 2 if n_row % 2 == 0 else 1
    n_high = n_row // n_low
    high, low = row // n_low, lax.rem(row, n_low)
    me = row * n_col + col
    size = src_ref.shape[0]
    own = tgt_ref.shape[0]

    def rows_of(q):
        return pl.ds(pl.multiple_of(q * size, size), size)

    def after(k):
        return lax.rem(me + k, n_dev)

    def before(k):
        return lax.rem(me - k + n_dev, n_dev)

    def peer(q):
        return {"row": q // n_col, "col": lax.rem(q, n_col)}

    def copy(src, dst, send, recv, device):
        return pltpu.make_async_remote_copy(
            src_ref=src, dst_ref=dst, send_sem=send, recv_sem=recv,
            device_id=device, device_id_type=MESH,
        )

    def gather_copy(q, origin, send):
        block = src_all.at[rows_of(origin), :]
        return copy(block, block, send, gather_recv.at[origin], peer(q))

    def sum_copy(q, origin):
        return copy(part.at[:, rows_of(q)], inbox.at[origin],
                    sum_send.at[q], sum_recv.at[origin], peer(q))

    def left_copy(q, origin):
        return copy(left.at[:, rows_of(origin)], left.at[:, rows_of(origin)],
                    left_send.at[q], left_recv.at[origin], peer(q))

    def normalise(emb_ref, scale_ref, out_ref, start, count):
        for j in range(count // 128):
            values = emb_ref[j * 128:(j + 1) * 128, :].astype(F32)
            squares = jnp.sum(values * values, axis=1, keepdims=True) + 1e-06
            scale = jnp.broadcast_to(scale_ref[:, j * 128:(j + 1) * 128], (128, 128)).T
            rows = pl.ds(pl.multiple_of(start + j * 128, 128), 128)
            out_ref[rows, :] = (values * (scale / jnp.sqrt(squares))).astype(BF16)

    barrier = pltpu.get_barrier_semaphore()

    @pl.loop(1, n_dev)
    def _(k):
        pl.semaphore_signal(barrier, inc=1, device_id=peer(after(k)), device_id_type=MESH)

    normalise(src_ref, src_scale_ref, src_all, me * size, size)
    pl.semaphore_wait(barrier, n_dev - 1)

    def at(high, low, column):
        return (high * n_low + low) * n_col + column

    def far_copy(k):
        q = at(lax.rem(high + k, n_high), low, col)
        return gather_copy(q, me, far_send.at[k])

    def low_copy(k, origin):
        q = at(high, lax.rem(low + k, n_low), col)
        return gather_copy(q, origin, low_send.at[k, origin])

    def col_copy(k, origin):
        q = at(high, low, lax.rem(col + k, n_col))
        return gather_copy(q, origin, col_send.at[k, origin])

    @pl.loop(1, n_high)
    def _(k):
        far_copy(k).start()

    for k in range(1, n_low):
        low_copy(k, me).start()
    for k in range(1, n_col):
        col_copy(k, me).start()

    normalise(tgt_ref, tgt_scale_ref, tgt_all, 0, own)

    def lane_sums(tile_of):
        acc = tile_of(0)
        for j in range(1, own // 128):
            acc = acc + tile_of(j)
        return acc

    def make_tile(block, q):
        scores = lax.dot_general(
            block, tgt_all[...], (((1,), (1,)), ((), ())), preferred_element_type=F32
        )
        tile = jnp.exp2(scores * (LOG2_E / EPSILON)).astype(BF16)
        kernel[rows_of(q), :] = tile
        tile = tile.astype(F32)
        acc = lane_sums(lambda j: tile[:, j * 128:(j + 1) * 128])
        return lanes_to_row(acc)[0:1, :]

    def weigh_tile(q):
        acc = lane_sums(
            lambda j: kernel[rows_of(q), j * 128:(j + 1) * 128].astype(F32)
            * right[:, j * 128:(j + 1) * 128]
        )
        return lanes_to_row(acc)[0:1, :]

    def finish_left():
        @pl.loop(1, n_dev)
        def _(k):
            q = before(k)
            sum_copy(q, q).wait_recv()

        total = jnp.sum(inbox[...], axis=0)
        mass = src_mass_ref[:, pl.ds(pl.multiple_of(col * size, size), size)]
        left[:, rows_of(me)] = mass / total

        @pl.loop(1, n_dev)
        def _(k):
            left_copy(after(k), me).start()

        @pl.loop(1, n_dev)
        def _(k):
            q = before(k)
            left_copy(q, q).wait_recv()

        @pl.loop(1, n_dev)
        def _(k):
            q = after(k)
            sum_copy(q, me).wait_send()
            left_copy(q, me).wait_send()

    def right_scaling():
        weights = jnp.broadcast_to(left[...].astype(BF16), (8, left.shape[1]))
        cols = jnp.dot(weights, kernel[...], preferred_element_type=F32)
        mass = tgt_mass_ref[:, pl.ds(pl.multiple_of(row * own, own), own)]
        return mass / cols[0:1, :]

    def use(origin):
        part[:, rows_of(origin)] = make_tile(src_all[rows_of(origin), :], origin)
        sum_copy(origin, me).start()

    inbox[me] = make_tile(src_all[rows_of(me), :], me)

    @pl.loop(1, n_high)
    def _(k):
        origin = at(lax.rem(high - k + n_high, n_high), low, col)
        gather_copy(origin, origin, far_send.at[k]).wait_recv()
        for j in range(1, n_low):
            low_copy(j, origin).start()
        for j in range(1, n_col):
            col_copy(j, origin).start()
        use(origin)

    for i in range(1, n_low):
        @pl.loop(0, n_high)
        def _(k):
            other = lax.rem(low - i + n_low, n_low)
            origin = at(lax.rem(high - k + n_high, n_high), other, col)
            gather_copy(origin, origin, far_send.at[0]).wait_recv()
            for j in range(1, n_col):
                col_copy(j, origin).start()
            use(origin)

    for i in range(1, n_col):
        for l in range(n_low):
            @pl.loop(0, n_high)
            def _(k):
                near = lax.rem(low - l + n_low, n_low)
                column = lax.rem(col - i + n_col, n_col)
                origin = at(lax.rem(high - k + n_high, n_high), near, column)
                gather_copy(origin, origin, far_send.at[0]).wait_recv()
                use(origin)

    @pl.loop(1, n_high)
    def _(k):
        far_copy(k).wait_send()

    @pl.loop(0, n_high)
    def _(h):
        for j in range(1, n_low):
            low_copy(j, at(h, low, col)).wait_send()
        for j in range(1, n_col):
            for l in range(n_low):
                col_copy(j, at(h, l, col)).wait_send()

    finish_left()

    @pl.loop(1, ITERS)
    def _(step):
        right[...] = right_scaling().astype(BF16).astype(F32)

        @pl.loop(1, n_dev)
        def _(k):
            q = before(k)
            part[:, rows_of(q)] = weigh_tile(q)
            sum_copy(q, me).start()

        inbox[me] = weigh_tile(me)
        finish_left()

    def out_block(r):
        return tgt_out.at[:, pl.ds(pl.multiple_of(r * own, own), own)]

    def out_copy(r, origin):
        return copy(out_block(origin), out_block(origin),
                    out_send.at[r], out_recv.at[origin], {"row": r, "col": col})

    tgt_out[:, pl.ds(pl.multiple_of(row * own, own), own)] = right_scaling()

    @pl.loop(1, n_row)
    def _(k):
        out_copy(lax.rem(row + k, n_row), row).start()

    span = n_col * size
    src_out[...] = left[:, pl.ds(pl.multiple_of(row * span, span), span)]

    @pl.loop(1, n_row)
    def _(k):
        r = lax.rem(row - k + n_row, n_row)
        out_copy(r, r).wait_recv()
        out_copy(lax.rem(row + k, n_row), row).wait_send()


def body(n_row, n_col, src_emb, tgt_emb, src_scale, tgt_scale, src_mass, tgt_mass):
    n_dev = n_row * n_col
    size, feat = src_emb.shape
    own = tgt_emb.shape[0]
    total = n_dev * size
    vmem = pl.BlockSpec(memory_space=pltpu.VMEM)
    dma = pltpu.SemaphoreType.DMA
    left, right = pl.pallas_call(
        functools.partial(sinkhorn, n_row, n_col),
        out_shape=(
            jax.ShapeDtypeStruct((1, n_col * size), F32),
            jax.ShapeDtypeStruct((1, n_row * own), F32),
        ),
        in_specs=[vmem] * 6,
        out_specs=(vmem, vmem),
        scratch_shapes=[
            pltpu.VMEM((total, feat), BF16),
            pltpu.VMEM((own, feat), BF16),
            pltpu.VMEM((total, own), BF16),
            pltpu.VMEM((1, total), F32),
            pltpu.VMEM((n_dev, 1, size), F32),
            pltpu.VMEM((1, total), F32),
            pltpu.VMEM((1, own), F32),
            dma((n_row,)), dma((2, n_dev)), dma((n_col, n_dev)), dma((n_dev,)),
            dma((n_dev,)), dma((n_dev,)), dma((n_dev,)), dma((n_dev,)),
            dma((n_row,)), dma((n_row,)),
        ],
        compiler_params=pltpu.CompilerParams(
            collective_id=0, has_side_effects=True, vmem_limit_bytes=56 * 2**20
        ),
        name="sinkhorn",
    )(
        src_emb, tgt_emb, src_scale[None, :], tgt_scale[None, :],
        src_mass[None, :], tgt_mass[None, :],
    )
    return EPSILON * jnp.log(left[0]), EPSILON * jnp.log(right[0])


def solution(mesh):
    in_specs = (
        P(("groups", "row", "col"), None),
        P(("groups", "col", "row"), None),
        P(("groups", "row", "col")),
        P(("groups", "col", "row")),
        P(("groups", "row")),
        P(("groups", "col")),
    )
    out_specs = (P(("groups", "row")), P(("groups", "col")))
    step = functools.partial(body, mesh.shape["row"], mesh.shape["col"])
    return jax.shard_map(step, mesh=mesh, in_specs=in_specs, out_specs=out_specs, check_vma=False)
```

```python
import functools
import jax
import jax.numpy as jnp
from jax import lax
from jax.experimental import pallas as pl
from jax.experimental.pallas import tpu as pltpu
from jax.sharding import PartitionSpec as P

ITERS = 3


EPSILON = 0.05
LOG2_E = 1.4426950408889634
MESH = pl.DeviceIdType.MESH
F32 = jnp.float32
BF16 = jnp.bfloat16


def whole_sums_fit(n_dev, total):
    return n_dev <= 16 and total % 4096 == 0


def lanes_to_row(acc):
    high = acc.astype(BF16)
    low = (acc - high.astype(F32)).astype(BF16)
    both = jnp.concatenate([high, low], axis=1)
    ones = jnp.ones((8, both.shape[1]), BF16)
    return lax.dot_general(
        ones, both, (((1,), (1,)), ((), ())), preferred_element_type=F32
    )


def sinkhorn(
    n_row, n_col,
    src_ref, tgt_ref, src_scale_ref, tgt_scale_ref, src_mass_ref, tgt_mass_ref,
    src_out, tgt_out,
    src_all, tgt_all, kernel, part, inbox, left, right,
    mass_all, part_rows, outbox, rows_inbox, mass_send, mass_recv, whole_send, whole_recv,
    far_send, low_send, col_send, gather_recv, sum_send, sum_recv, left_send, left_recv, out_send, out_recv,
):
    n_dev = n_row * n_col
    unroll = n_dev - 1 if n_dev <= 16 else 1

    def wrap(i, n):
        return jnp.where(i >= n, i - n, i)

    row, col = lax.axis_index("row"), lax.axis_index("col")
    n_low = 2 if n_row % 2 == 0 else 1
    n_high = n_row // n_low
    high, low = row // n_low, lax.rem(row, n_low)
    me = row * n_col + col
    size = src_ref.shape[0]
    own = tgt_ref.shape[0]

    def rows_of(q):
        return pl.ds(pl.multiple_of(q * size, size), size)

    def after(k):
        return wrap(me + k, n_dev)

    def before(k):
        return wrap(me - k + n_dev, n_dev)

    def peer(q):
        return {"row": q // n_col, "col": lax.rem(q, n_col)}

    def copy(src, dst, send, recv, device):
        return pltpu.make_async_remote_copy(
            src_ref=src, dst_ref=dst, send_sem=send, recv_sem=recv,
            device_id=device, device_id_type=MESH,
        )

    def gather_copy(q, origin, send):
        block = src_all.at[rows_of(origin), :]
        return copy(block, block, send, gather_recv.at[origin], peer(q))

    def sum_copy(q, origin):
        return copy(part.at[:, rows_of(q)], inbox.at[origin], sum_send, sum_recv, peer(q))

    def all_sums():
        others = inbox.at[pl.ds(0, n_dev - 1)]
        return copy(others, others, sum_send, sum_recv, peer(after(1)))

    whole_sums = whole_sums_fit(n_dev, n_dev * size)
    lines = n_dev * size // 128
    half = lines // 2

    def whole_copy(q, origin, h, turn):
        rows = pl.ds(h * half, half)
        return copy(outbox.at[rows, :], rows_inbox.at[turn, origin, rows, :],
                    whole_send.at[turn], whole_recv.at[turn], peer(q))

    def all_wholes(turn):
        others = rows_inbox.at[turn, pl.ds(0, n_dev - 1)]
        return copy(others, others, whole_send.at[turn], whole_recv.at[turn], peer(after(1)))

    def send_half(h, turn):
        rows = slice(h * half, (h + 1) * half)
        outbox[rows, :] = part_rows[rows, :].astype(BF16)

        @pl.loop(1, n_dev, unroll=unroll)
        def _(k):
            whole_copy(after(k), me, h, turn).start()

    def put_sums(q, sums):
        if whole_sums:
            for j in range(size // 128):
                part_rows[pl.ds(q * (size // 128) + j, 1), :] = sums[:, j * 128:(j + 1) * 128]
        else:
            part[:, rows_of(q)] = sums
            sum_copy(q, me).start()

    def mass_copy(r, origin):
        span = n_col * size
        block = mass_all.at[:, pl.ds(pl.multiple_of(origin * span, span), span)]
        return copy(src_mass_ref, block, mass_send, mass_recv, {"row": r, "col": col})

    def all_masses():
        others = mass_all.at[:, pl.ds(0, (n_row - 1) * n_col * size)]
        return copy(others, others, mass_send, mass_recv,
                    {"row": wrap(row + 1, n_row), "col": col})

    def all_lefts():
        others = left.at[:, pl.ds(0, (n_dev - 1) * size)]
        return copy(others, others, left_send, left_recv, peer(after(1)))

    def left_copy(q, origin):
        return copy(left.at[:, rows_of(origin)], left.at[:, rows_of(origin)],
                    left_send, left_recv, peer(q))

    def normalise(emb_ref, scale_ref, out_ref, start, count):
        for j in range(count // 128):
            values = emb_ref[j * 128:(j + 1) * 128, :].astype(F32)
            squares = jnp.sum(values * values, axis=1, keepdims=True) + 1e-06
            scale = jnp.broadcast_to(scale_ref[:, j * 128:(j + 1) * 128], (128, 128)).T
            rows = pl.ds(pl.multiple_of(start + j * 128, 128), 128)
            out_ref[rows, :] = (values * (scale / jnp.sqrt(squares))).astype(BF16)

    barrier = pltpu.get_barrier_semaphore()

    @pl.loop(1, n_dev, unroll=unroll)
    def _(k):
        pl.semaphore_signal(barrier, inc=1, device_id=peer(after(k)), device_id_type=MESH)

    normalise(src_ref, src_scale_ref, src_all, me * size, size)
    pl.semaphore_wait(barrier, n_dev - 1)

    def at(high, low, column):
        return (high * n_low + low) * n_col + column

    def far_copy(k):
        q = at(lax.rem(high + k, n_high), low, col)
        return gather_copy(q, me, far_send.at[k])

    def low_copy(k, origin):
        q = at(high, lax.rem(low + k, n_low), col)
        return gather_copy(q, origin, low_send.at[k, origin])

    def col_copy(k, origin):
        q = at(high, low, lax.rem(col + k, n_col))
        return gather_copy(q, origin, col_send.at[k, origin])

    @pl.loop(1, n_high)
    def _(k):
        far_copy(k).start()

    for k in range(1, n_low):
        low_copy(k, me).start()
    for k in range(1, n_col):
        col_copy(k, me).start()

    if whole_sums:
        span = n_col * size
        mass_all[:, pl.ds(pl.multiple_of(row * span, span), span)] = src_mass_ref[...]

        @pl.loop(1, n_row)
        def _(k):
            mass_copy(wrap(row + k, n_row), row).start()

    normalise(tgt_ref, tgt_scale_ref, tgt_all, 0, own)

    def lane_sums(tile_of):
        acc = tile_of(0)
        for j in range(1, own // 128):
            acc = acc + tile_of(j)
        return acc

    def make_tile(block, q):
        scores = lax.dot_general(
            block, tgt_all[...], (((1,), (1,)), ((), ())), preferred_element_type=F32
        )
        tile = jnp.exp2(scores * (LOG2_E / EPSILON)).astype(BF16)
        kernel[rows_of(q), :] = tile
        tile = tile.astype(F32)
        acc = lane_sums(lambda j: tile[:, j * 128:(j + 1) * 128])
        return lanes_to_row(acc)[0:1, :]

    def weigh_tile(q):
        acc = lane_sums(
            lambda j: kernel[rows_of(q), j * 128:(j + 1) * 128].astype(F32)
            * right[:, j * 128:(j + 1) * 128]
        )
        return lanes_to_row(acc)[0:1, :]

    def finish_left(turn):
        if whole_sums:
            rows_inbox[turn, me] = part_rows[...].astype(BF16)
            all_wholes(turn).wait()
            part_rows[...] = jnp.sum(rows_inbox[turn].astype(F32), axis=0)
            for j in range(lines):
                lanes = slice(j * 128, (j + 1) * 128)
                left[:, lanes] = mass_all[:, lanes] / part_rows[j:j + 1, :]
            return
        all_sums().wait_recv()
        total = jnp.sum(inbox[...], axis=0)
        mass = src_mass_ref[:, pl.ds(pl.multiple_of(col * size, size), size)]
        left[:, rows_of(me)] = mass / total

        @pl.loop(1, n_dev, unroll=unroll)
        def _(k):
            left_copy(after(k), me).start()

        all_lefts().wait()
        all_sums().wait_send()

    def right_scaling():
        weights = jnp.broadcast_to(left[...].astype(BF16), (8, left.shape[1]))
        cols = jnp.dot(weights, kernel[...], preferred_element_type=F32)
        mass = tgt_mass_ref[:, pl.ds(pl.multiple_of(row * own, own), own)]
        return mass / cols[0:1, :]

    def use(origin):
        put_sums(origin, make_tile(src_all[rows_of(origin), :], origin))

    if whole_sums:
        put_sums(me, make_tile(src_all[rows_of(me), :], me))
    else:
        inbox[me] = make_tile(src_all[rows_of(me), :], me)

    @pl.loop(1, n_high)
    def _(k):
        origin = at(lax.rem(high - k + n_high, n_high), low, col)
        gather_copy(origin, origin, far_send.at[k]).wait_recv()
        for j in range(1, n_low):
            low_copy(j, origin).start()
        for j in range(1, n_col):
            col_copy(j, origin).start()
        use(origin)

    for i in range(1, n_low):
        @pl.loop(0, n_high)
        def _(k):
            other = lax.rem(low - i + n_low, n_low)
            origin = at(lax.rem(high - k + n_high, n_high), other, col)
            gather_copy(origin, origin, far_send.at[0]).wait_recv()
            for j in range(1, n_col):
                col_copy(j, origin).start()
            use(origin)

    for i in range(1, n_col):
        for l in range(n_low):
            @pl.loop(0, n_high)
            def _(k):
                near = lax.rem(low - l + n_low, n_low)
                column = lax.rem(col - i + n_col, n_col)
                origin = at(lax.rem(high - k + n_high, n_high), near, column)
                gather_copy(origin, origin, far_send.at[0]).wait_recv()
                use(origin)

    if whole_sums:
        send_half(0, 0)
        send_half(1, 0)
        all_masses().wait()

    @pl.loop(1, n_high)
    def _(k):
        far_copy(k).wait_send()

    @pl.loop(0, n_high)
    def _(h):
        for j in range(1, n_low):
            low_copy(j, at(h, low, col)).wait_send()
        for j in range(1, n_col):
            for l in range(n_low):
                col_copy(j, at(h, l, col)).wait_send()

    finish_left(0)

    @pl.loop(1, ITERS)
    def _(step):
        turn = lax.rem(step, 2)
        right[...] = right_scaling().astype(BF16).astype(F32)

        if whole_sums:
            for h in range(2):
                @pl.loop(h * (n_dev // 2), (h + 1) * (n_dev // 2))
                def _(q):
                    put_sums(q, weigh_tile(q))

                send_half(h, turn)
        else:
            @pl.loop(1, n_dev)
            def _(k):
                q = before(k)
                put_sums(q, weigh_tile(q))

            inbox[me] = weigh_tile(me)
        finish_left(turn)

    def out_block(r):
        return tgt_out.at[:, pl.ds(pl.multiple_of(r * own, own), own)]

    def out_copy(r, origin):
        return copy(out_block(origin), out_block(origin),
                    out_send, out_recv, {"row": r, "col": col})

    def all_outs():
        others = tgt_out.at[:, pl.ds(0, (n_row - 1) * own)]
        return copy(others, others, out_send, out_recv, {"row": wrap(row + 1, n_row), "col": col})

    tgt_out[:, pl.ds(pl.multiple_of(row * own, own), own)] = right_scaling()

    @pl.loop(1, n_row, unroll=min(unroll, n_row - 1))
    def _(k):
        out_copy(wrap(row + k, n_row), row).start()

    span = n_col * size
    src_out[...] = left[:, pl.ds(pl.multiple_of(row * span, span), span)]

    all_outs().wait()


def body(n_row, n_col, src_emb, tgt_emb, src_scale, tgt_scale, src_mass, tgt_mass):
    n_dev = n_row * n_col
    size, feat = src_emb.shape
    own = tgt_emb.shape[0]
    total = n_dev * size
    whole_sums = whole_sums_fit(n_dev, total)
    lines = total // 128 if whole_sums else 16
    vmem = pl.BlockSpec(memory_space=pltpu.VMEM)
    dma = pltpu.SemaphoreType.DMA
    left, right = pl.pallas_call(
        functools.partial(sinkhorn, n_row, n_col),
        out_shape=(
            jax.ShapeDtypeStruct((1, n_col * size), F32),
            jax.ShapeDtypeStruct((1, n_row * own), F32),
        ),
        in_specs=[vmem] * 6,
        out_specs=(vmem, vmem),
        scratch_shapes=[
            pltpu.VMEM((total, feat), BF16),
            pltpu.VMEM((own, feat), BF16),
            pltpu.VMEM((total, own), BF16),
            pltpu.VMEM((1, total), F32),
            pltpu.VMEM((n_dev, 1, size), F32),
            pltpu.VMEM((1, total), F32),
            pltpu.VMEM((1, own), F32),
            pltpu.VMEM((1, total if whole_sums else 128), F32),
            pltpu.VMEM((lines, 128), F32),
            pltpu.VMEM((lines, 128), BF16),
            pltpu.VMEM((2, n_dev if whole_sums else 1, lines, 128), BF16),
            dma, dma, dma((2,)), dma((2,)),
            dma((n_row,)), dma((2, n_dev)), dma((n_col, n_dev)), dma((n_dev,)),
            dma, dma, dma, dma, dma, dma,
        ],
        compiler_params=pltpu.CompilerParams(
            collective_id=0, has_side_effects=True, vmem_limit_bytes=56 * 2**20
        ),
        name="sinkhorn",
    )(
        src_emb, tgt_emb, src_scale[None, :], tgt_scale[None, :],
        src_mass[None, :], tgt_mass[None, :],
    )
    return EPSILON * jnp.log(left[0]), EPSILON * jnp.log(right[0])


def solution(mesh):
    in_specs = (
        P(("groups", "row", "col"), None),
        P(("groups", "col", "row"), None),
        P(("groups", "row", "col")),
        P(("groups", "col", "row")),
        P(("groups", "row")),
        P(("groups", "col")),
    )
    out_specs = (P(("groups", "row")), P(("groups", "col")))
    step = functools.partial(body, mesh.shape["row"], mesh.shape["col"])
    return jax.shard_map(step, mesh=mesh, in_specs=in_specs, out_specs=out_specs, check_vma=False)
```

```python
import functools
import jax
import jax.numpy as jnp
from jax import lax
from jax.experimental import pallas as pl
from jax.experimental.pallas import tpu as pltpu
from jax.sharding import PartitionSpec as P

ITERS = 3


EPSILON = 0.05
LOG2_E = 1.4426950408889634
MESH = pl.DeviceIdType.MESH
F32 = jnp.float32
BF16 = jnp.bfloat16


def whole_sums_fit(n_dev, total):
    return n_dev <= 16 and total % 4096 == 0


def lanes_to_row(acc):
    high = acc.astype(BF16)
    low = (acc - high.astype(F32)).astype(BF16)
    both = jnp.concatenate([high, low], axis=1)
    ones = jnp.ones((8, both.shape[1]), BF16)
    return lax.dot_general(
        ones, both, (((1,), (1,)), ((), ())), preferred_element_type=F32
    )


def sinkhorn(
    n_row, n_col,
    src_ref, tgt_ref, src_scale_ref, tgt_scale_ref, src_mass_ref, tgt_mass_ref,
    src_out, tgt_out,
    src_all, tgt_all, kernel, part, inbox, left, right,
    mass_all, part_rows, outbox, rows_inbox, mass_send, mass_recv, whole_send, whole_recv,
    far_send, low_send, col_send, gather_recv, sum_send, sum_recv, left_send, left_recv, out_send, out_recv,
):
    n_dev = n_row * n_col
    unroll = n_dev - 1 if n_dev <= 16 else 1

    def wrap(i, n):
        return jnp.where(i >= n, i - n, i)

    row, col = lax.axis_index("row"), lax.axis_index("col")
    n_low = 2 if n_row % 2 == 0 else 1
    n_high = n_row // n_low
    high, low = row // n_low, lax.rem(row, n_low)
    me = row * n_col + col
    size = src_ref.shape[0]
    own = tgt_ref.shape[0]

    def rows_of(q):
        return pl.ds(pl.multiple_of(q * size, size), size)

    def after(k):
        return wrap(me + k, n_dev)

    def before(k):
        return wrap(me - k + n_dev, n_dev)

    def peer(q):
        return {"row": q // n_col, "col": lax.rem(q, n_col)}

    def copy(src, dst, send, recv, device):
        return pltpu.make_async_remote_copy(
            src_ref=src, dst_ref=dst, send_sem=send, recv_sem=recv,
            device_id=device, device_id_type=MESH,
        )

    def gather_copy(q, origin, send):
        block = src_all.at[rows_of(origin), :]
        return copy(block, block, send, gather_recv.at[origin], peer(q))

    def sum_copy(q, origin):
        return copy(part.at[:, rows_of(q)], inbox.at[origin], sum_send, sum_recv, peer(q))

    def all_sums():
        others = inbox.at[pl.ds(0, n_dev - 1)]
        return copy(others, others, sum_send, sum_recv, peer(after(1)))

    whole_sums = whole_sums_fit(n_dev, n_dev * size)
    lines = n_dev * size // 128
    half = lines // 2

    def whole_copy(q, origin, h, turn):
        rows = pl.ds(h * half, half)
        return copy(outbox.at[rows, :], rows_inbox.at[turn, origin, rows, :],
                    whole_send.at[turn], whole_recv.at[turn], peer(q))

    def all_wholes(turn):
        others = rows_inbox.at[turn, pl.ds(0, n_dev - 1)]
        return copy(others, others, whole_send.at[turn], whole_recv.at[turn], peer(after(1)))

    def send_half(h, turn):
        rows = slice(h * half, (h + 1) * half)
        outbox[rows, :] = part_rows[rows, :].astype(BF16)

        @pl.loop(1, n_dev, unroll=unroll)
        def _(k):
            whole_copy(after(k), me, h, turn).start()

    def put_sums(q, sums):
        if whole_sums:
            for j in range(size // 128):
                part_rows[pl.ds(q * (size // 128) + j, 1), :] = sums[:, j * 128:(j + 1) * 128]
        else:
            part[:, rows_of(q)] = sums
            sum_copy(q, me).start()

    def mass_copy(r, origin):
        span = n_col * size
        block = mass_all.at[:, pl.ds(pl.multiple_of(origin * span, span), span)]
        return copy(src_mass_ref, block, mass_send, mass_recv, {"row": r, "col": col})

    def all_masses():
        others = mass_all.at[:, pl.ds(0, (n_row - 1) * n_col * size)]
        return copy(others, others, mass_send, mass_recv,
                    {"row": wrap(row + 1, n_row), "col": col})

    def all_lefts():
        others = left.at[:, pl.ds(0, (n_dev - 1) * size)]
        return copy(others, others, left_send, left_recv, peer(after(1)))

    def left_copy(q, origin):
        return copy(left.at[:, rows_of(origin)], left.at[:, rows_of(origin)],
                    left_send, left_recv, peer(q))

    def normalise(emb_ref, scale_ref, out_ref, start, count):
        for j in range(count // 128):
            values = emb_ref[j * 128:(j + 1) * 128, :].astype(F32)
            squares = jnp.sum(values * values, axis=1, keepdims=True) + 1e-06
            scale = jnp.broadcast_to(scale_ref[:, j * 128:(j + 1) * 128], (128, 128)).T
            rows = pl.ds(pl.multiple_of(start + j * 128, 128), 128)
            out_ref[rows, :] = (values * (scale / jnp.sqrt(squares))).astype(BF16)

    barrier = pltpu.get_barrier_semaphore()

    @pl.loop(1, n_dev, unroll=unroll)
    def _(k):
        pl.semaphore_signal(barrier, inc=1, device_id=peer(after(k)), device_id_type=MESH)

    normalise(src_ref, src_scale_ref, src_all, me * size, size)
    pl.semaphore_wait(barrier, n_dev - 1)

    def at(high, low, column):
        return (high * n_low + low) * n_col + column

    def far_copy(k):
        q = at(lax.rem(high + k, n_high), low, col)
        return gather_copy(q, me, far_send.at[k])

    def low_copy(k, origin):
        q = at(high, lax.rem(low + k, n_low), col)
        return gather_copy(q, origin, low_send.at[k, origin])

    def col_copy(k, origin):
        q = at(high, low, lax.rem(col + k, n_col))
        return gather_copy(q, origin, col_send.at[k, origin])

    @pl.loop(1, n_high)
    def _(k):
        far_copy(k).start()

    for k in range(1, n_low):
        low_copy(k, me).start()
    for k in range(1, n_col):
        col_copy(k, me).start()

    if whole_sums:
        span = n_col * size
        mass_all[:, pl.ds(pl.multiple_of(row * span, span), span)] = src_mass_ref[...]

        @pl.loop(1, n_row)
        def _(k):
            mass_copy(wrap(row + k, n_row), row).start()

    normalise(tgt_ref, tgt_scale_ref, tgt_all, 0, own)

    def lane_sums(tile_of):
        acc = tile_of(0)
        for j in range(1, own // 128):
            acc = acc + tile_of(j)
        return acc

    def make_tile(block, q):
        scores = lax.dot_general(
            block, tgt_all[...], (((1,), (1,)), ((), ())), preferred_element_type=F32
        )
        tile = jnp.exp2(scores * (LOG2_E / EPSILON)).astype(BF16)
        kernel[rows_of(q), :] = tile
        tile = tile.astype(F32)
        acc = lane_sums(lambda j: tile[:, j * 128:(j + 1) * 128])
        return lanes_to_row(acc)[0:1, :]

    def weigh_tile(q):
        acc = lane_sums(
            lambda j: kernel[rows_of(q), j * 128:(j + 1) * 128].astype(F32)
            * right[:, j * 128:(j + 1) * 128]
        )
        return lanes_to_row(acc)[0:1, :]

    def finish_left(turn):
        if whole_sums:
            rows_inbox[turn, me] = part_rows[...].astype(BF16)
            all_wholes(turn).wait()
            part_rows[...] = jnp.sum(rows_inbox[turn].astype(F32), axis=0)
            for j in range(lines):
                lanes = slice(j * 128, (j + 1) * 128)
                left[:, lanes] = mass_all[:, lanes] / part_rows[j:j + 1, :]
            return
        all_sums().wait_recv()
        total = jnp.sum(inbox[...], axis=0)
        mass = src_mass_ref[:, pl.ds(pl.multiple_of(col * size, size), size)]
        left[:, rows_of(me)] = mass / total

        @pl.loop(1, n_dev, unroll=unroll)
        def _(k):
            left_copy(after(k), me).start()

        all_lefts().wait()
        all_sums().wait_send()

    def right_scaling():
        weights = jnp.broadcast_to(left[...].astype(BF16), (8, left.shape[1]))
        cols = jnp.dot(weights, kernel[...], preferred_element_type=F32)
        mass = tgt_mass_ref[:, pl.ds(pl.multiple_of(row * own, own), own)]
        return mass / cols[0:1, :]

    def use(origin):
        put_sums(origin, make_tile(src_all[rows_of(origin), :], origin))

    if whole_sums:
        put_sums(me, make_tile(src_all[rows_of(me), :], me))
    else:
        inbox[me] = make_tile(src_all[rows_of(me), :], me)

    @pl.loop(1, n_high)
    def _(k):
        origin = at(lax.rem(high - k + n_high, n_high), low, col)
        gather_copy(origin, origin, far_send.at[k]).wait_recv()
        for j in range(1, n_low):
            low_copy(j, origin).start()
        for j in range(1, n_col):
            col_copy(j, origin).start()
        use(origin)

    for i in range(1, n_low):
        @pl.loop(0, n_high)
        def _(k):
            other = lax.rem(low - i + n_low, n_low)
            origin = at(lax.rem(high - k + n_high, n_high), other, col)
            gather_copy(origin, origin, far_send.at[0]).wait_recv()
            for j in range(1, n_col):
                col_copy(j, origin).start()
            use(origin)

    for i in range(1, n_col):
        for l in range(n_low):
            @pl.loop(0, n_high)
            def _(k):
                near = lax.rem(low - l + n_low, n_low)
                column = lax.rem(col - i + n_col, n_col)
                origin = at(lax.rem(high - k + n_high, n_high), near, column)
                gather_copy(origin, origin, far_send.at[0]).wait_recv()
                use(origin)

    if whole_sums:
        send_half(0, 0)
        send_half(1, 0)
        all_masses().wait()

    @pl.loop(1, n_high)
    def _(k):
        far_copy(k).wait_send()

    @pl.loop(0, n_high)
    def _(h):
        for j in range(1, n_low):
            low_copy(j, at(h, low, col)).wait_send()
        for j in range(1, n_col):
            for l in range(n_low):
                col_copy(j, at(h, l, col)).wait_send()

    finish_left(0)

    @pl.loop(1, ITERS)
    def _(step):
        turn = lax.rem(step, 2)
        right[...] = right_scaling().astype(BF16).astype(F32)

        if whole_sums:
            for h in range(2):
                @pl.loop(h * (n_dev // 2), (h + 1) * (n_dev // 2), unroll=8)
                def _(q):
                    put_sums(q, weigh_tile(q))

                send_half(h, turn)
        else:
            @pl.loop(1, n_dev)
            def _(k):
                q = before(k)
                put_sums(q, weigh_tile(q))

            inbox[me] = weigh_tile(me)
        finish_left(turn)

    def out_block(r):
        return tgt_out.at[:, pl.ds(pl.multiple_of(r * own, own), own)]

    def out_copy(r, origin):
        return copy(out_block(origin), out_block(origin),
                    out_send, out_recv, {"row": r, "col": col})

    def all_outs():
        others = tgt_out.at[:, pl.ds(0, (n_row - 1) * own)]
        return copy(others, others, out_send, out_recv, {"row": wrap(row + 1, n_row), "col": col})

    tgt_out[:, pl.ds(pl.multiple_of(row * own, own), own)] = right_scaling()

    @pl.loop(1, n_row, unroll=min(unroll, n_row - 1))
    def _(k):
        out_copy(wrap(row + k, n_row), row).start()

    span = n_col * size
    src_out[...] = left[:, pl.ds(pl.multiple_of(row * span, span), span)]

    all_outs().wait()


def body(n_row, n_col, src_emb, tgt_emb, src_scale, tgt_scale, src_mass, tgt_mass):
    n_dev = n_row * n_col
    size, feat = src_emb.shape
    own = tgt_emb.shape[0]
    total = n_dev * size
    whole_sums = whole_sums_fit(n_dev, total)
    lines = total // 128 if whole_sums else 16
    vmem = pl.BlockSpec(memory_space=pltpu.VMEM)
    dma = pltpu.SemaphoreType.DMA
    left, right = pl.pallas_call(
        functools.partial(sinkhorn, n_row, n_col),
        out_shape=(
            jax.ShapeDtypeStruct((1, n_col * size), F32),
            jax.ShapeDtypeStruct((1, n_row * own), F32),
        ),
        in_specs=[vmem] * 6,
        out_specs=(vmem, vmem),
        scratch_shapes=[
            pltpu.VMEM((total, feat), BF16),
            pltpu.VMEM((own, feat), BF16),
            pltpu.VMEM((total, own), BF16),
            pltpu.VMEM((1, total), F32),
            pltpu.VMEM((n_dev, 1, size), F32),
            pltpu.VMEM((1, total), F32),
            pltpu.VMEM((1, own), F32),
            pltpu.VMEM((1, total if whole_sums else 128), F32),
            pltpu.VMEM((lines, 128), F32),
            pltpu.VMEM((lines, 128), BF16),
            pltpu.VMEM((2, n_dev if whole_sums else 1, lines, 128), BF16),
            dma, dma, dma((2,)), dma((2,)),
            dma((n_row,)), dma((2, n_dev)), dma((n_col, n_dev)), dma((n_dev,)),
            dma, dma, dma, dma, dma, dma,
        ],
        compiler_params=pltpu.CompilerParams(
            collective_id=0, has_side_effects=True, vmem_limit_bytes=56 * 2**20
        ),
        name="sinkhorn",
    )(
        src_emb, tgt_emb, src_scale[None, :], tgt_scale[None, :],
        src_mass[None, :], tgt_mass[None, :],
    )
    return EPSILON * jnp.log(left[0]), EPSILON * jnp.log(right[0])


def solution(mesh):
    in_specs = (
        P(("groups", "row", "col"), None),
        P(("groups", "col", "row"), None),
        P(("groups", "row", "col")),
        P(("groups", "col", "row")),
        P(("groups", "row")),
        P(("groups", "col")),
    )
    out_specs = (P(("groups", "row")), P(("groups", "col")))
    step = functools.partial(body, mesh.shape["row"], mesh.shape["col"])
    return jax.shard_map(step, mesh=mesh, in_specs=in_specs, out_specs=out_specs, check_vma=False)
```
